512 devices in a mesh: sec: 4 (over y), ep: 128 (over x, z, core).
Axes of the slice: x: 4, y: 4, z: 16, core: 2. Of those that a mesh axis runs over, the one named last changes fastest.
Arguments:
- tokens: bfloat16 [2048, 3584], P('ep', 'sec'), may hold values from -6 to 6
- up_weight: bfloat16 [128, 3584, 1024], P('ep', 'sec'), may hold values from -0.09375 to 0.09375
- down_weight: bfloat16 [128, 1024, 3584], P('ep', None, 'sec'), may hold values from -0.1875 to 0.1875
- expert_ids: int32 [2048, 8], P('ep'), may hold values from 0 to 127, all different within a row; in each aligned block of 16 rows (0 to 15, 16 to 31, ...) at most 2 rows name the same one
- route_weight: float32 [2048, 8], P('ep'), may hold values from 0.05 to 1
Outputs:
- combined: bfloat16 [2048, 3584], P('ep', 'sec')
The draws below stay inside these ranges and needn't reach their ends.
Inputs may be any that keep to these rules, and one draw needn't show every extreme that they name: `expert_ids`: each token names 8 different experts. Among the tokens of one index of ep no expert is named more than 2 times, and that count is reached.
All inputs are finite; a program needn't handle non-finite values.
Results may differ from the reference program's by a relative error of at most 0.0058.
Values may be sent and summed in bfloat16 or wider, within the bound.
A program may use at most 64 MiB of HBM per device.

```python
import math
import jax
import jax.numpy as jnp
import numpy as np
from jax import lax

D = 3584
H = 1024
TOP = 8
TOK_DEV = 16
EXPERTS = 128
TOKENS = 2048
CAP = 2


def shard_levels(stream_key, shape, shards, smallest, largest):
    gain, own = 1.0, jax.random.fold_in(stream_key, 6)
    for dim, parts in shards:
        heights = jnp.exp(jax.random.uniform(jax.random.fold_in(own, dim), (parts,), jnp.float32, smallest / len(shards), largest / len(shards)))
        gain = gain * jnp.repeat(heights, shape[dim] // parts).reshape([-1 if axis == dim else 1 for axis in range(len(shape))])
    return gain


def deal_out(stream_key, own, number, rows, count, top, limit, slope):
    order = jax.random.permutation(stream_key, count)
    packed, usual = shares(count, rows * top, limit, slope, True), shares(count, rows * top, limit, slope, False)
    places = jnp.arange(count)

    def named(lengths, rotation):
        used = int((lengths > 0).sum())
        fixed = max(1, used // 4)
        shifted = fixed + (places - fixed + rotation * (used - fixed)) % max(1, count - fixed)
        return jnp.zeros((count,), jnp.int32).at[order[jnp.where(places < fixed, places, shifted)]].set(jnp.asarray(lengths, jnp.int32))

    lengths = jnp.where(number % 4 == 0, named(packed, number // 4), named(usual, number - number // 4 - 1))
    mixed = jax.random.permutation(jax.random.fold_in(own, 3), count)
    donor, receiver = mixed[0:count // 2 * 2:2], mixed[1:count // 2 * 2:2]
    slack = jnp.minimum(lengths[donor] - 1, limit - lengths[receiver]) // 2
    slack = jnp.where((donor == order[0]) | (receiver == order[0]) | (lengths[receiver] == 0), 0, jnp.maximum(slack, 0))
    shifted = jax.random.randint(jax.random.fold_in(own, 4), (count // 2,), 0, 1 << 20) % (slack + 1)
    lengths = lengths.at[donor].add(-shifted).at[receiver].add(shifted)
    items = jnp.searchsorted(jnp.cumsum(lengths), jnp.arange(rows * top), side="right").astype(jnp.int32)
    table = items.reshape(top, rows).T
    table = table[jax.random.permutation(jax.random.fold_in(own, 1), rows)]
    rotation = jax.random.randint(jax.random.fold_in(own, 2), (rows, 1), 0, top)
    return jnp.take_along_axis(table, (jnp.arange(top)[None, :] + rotation) % top, axis=1)


def shares(amount, total, limit, lean, full):
    portions = [(1 << 20) // math.isqrt(rank ** lean) + 1 for rank in range(1, amount + 1)]
    largest = limit if full else min(limit, max(-(-total // amount), total * portions[0] // sum(portions)))
    least = 1 if total - largest >= amount - 1 else 0
    counts, spare = [largest] + [least] * (amount - 1), total - largest - least * (amount - 1)
    while spare > 0:
        movable = [i for i in range(1, amount) if counts[i] < largest] or [i for i in range(1, amount) if counts[i] < limit]
        pool, left = sum([portions[i] for i in movable]), spare
        for i in movable:
            addition = min(limit - counts[i], max(1, left * portions[i] // pool), spare)
            counts[i] = counts[i] + addition
            spare = spare - addition
    return np.array(counts)


def normal_values(own_key, shape, spread, limit, pieces=(), kind=jnp.bfloat16):
    result = spread * jax.random.normal(own_key, shape, jnp.float32)
    if pieces:
        result = result * shard_levels(own_key, shape, pieces, -0.22, 0.18)
    return jnp.clip(result, -limit, limit).astype(kind)


def setup_inputs(seed: int = 0) -> dict:
    arg_keys = jax.random.split(jax.random.key(seed), 6)
    tokens = normal_values(arg_keys[0], (TOKENS, D), 1.0, 6.0, ((0, 128), (1, 4)))
    up_weight = normal_values(arg_keys[1], (EXPERTS, D, H), D ** -0.5, 0.09375, ((0, 128), (1, 4)))
    down_weight = normal_values(arg_keys[2], (EXPERTS, H, D), H ** -0.5, 0.1875, ((0, 128), (2, 4)))
    expert_ids_keys = jax.random.split(jax.random.fold_in(arg_keys[3], 1), TOKENS // TOK_DEV)
    expert_ids_turns = jax.random.permutation(jax.random.fold_in(arg_keys[3], 3), TOKENS // TOK_DEV)
    expert_ids = jax.vmap(lambda own, number: deal_out(jax.random.fold_in(arg_keys[3], 2), own, number, TOK_DEV, EXPERTS, TOP, CAP, 2))(expert_ids_keys, expert_ids_turns).reshape((TOKENS, TOP))
    route_weight = jnp.clip(jnp.exp(math.log(1.0) - 2.9957323 * jax.random.uniform(arg_keys[4], (TOKENS, TOP), jnp.float32) ** shard_levels(arg_keys[4], (TOKENS, TOP), ((0, 128),), -0.2, 0.2)), 0.05, 1.0)
    return {"tokens": tokens, "up_weight": up_weight, "down_weight": down_weight, "expert_ids": expert_ids, "route_weight": route_weight}


def reference(tokens, up_weight, down_weight, expert_ids, route_weight):
    flat_ids = expert_ids.reshape(-1)
    scale = 2.5 * route_weight / jnp.sum(route_weight, axis=1, keepdims=True)
    flat_scale = scale.reshape(-1)
    bound = EXPERTS * CAP

    def expert_step(total, inputs):
        up_matrix, down_matrix, number = inputs
        match = flat_ids == number
        order = jnp.argsort(jnp.where(match, 0, 1).astype(jnp.int32), stable=True)[:bound]
        live = match[order]
        token_rows = (order // TOP).astype(jnp.int32)
        gathered = tokens[token_rows]
        upper = jnp.dot(gathered, up_matrix, preferred_element_type=jnp.float32)
        activated = jax.nn.silu(upper).astype(jnp.bfloat16)
        expert_out = jnp.dot(activated, down_matrix, preferred_element_type=jnp.float32).astype(jnp.bfloat16)
        factor = jnp.where(live, flat_scale[order], jnp.zeros_like(flat_scale[order]))
        total = total.at[token_rows].add(factor[:, None] * expert_out.astype(jnp.float32))
        return total, None

    start = jnp.zeros((TOKENS, D), jnp.float32)
    total, unused = lax.scan(expert_step, start, (up_weight, down_weight, jnp.arange(EXPERTS, dtype=jnp.int32)))
    return total.astype(jnp.bfloat16)
```

```python
import functools

import jax
import jax.numpy as jnp
from jax import lax
from jax.experimental import pallas as pl
from jax.experimental.pallas import tpu as pltpu
from jax.sharding import PartitionSpec as P

MESH = pl.DeviceIdType.MESH
F32, BF16 = jnp.float32, jnp.bfloat16
NX, NY, NZ, NC = 4, 4, 16, 2
ROWS, TOP, CAP = 16, 8, 2
PLANE = NX * NC
ORDER = (0, 1, -1, 3, -3, 2, -2, 4, -4, 5, -5, 6, -6, 7, -7, 8)
PLACE = {o: i for i, o in enumerate(ORDER)}
FAR = (6, -6, 3, -3)
NEAR = tuple((a, b, 0) for a in (0, 3, -3, 6, -6) for b in (1, -1)) + ((6, 2, 1), (-6, -2, 2))
EARLY = tuple(a + b for a, b, _ in NEAR if a in (0, 3, -3))
PEERS_Z = (6, -6, 3, -3, 1, -1, 2, -2)


def offset(a, b):
    o = a + b
    return 8 if o == -8 else o


def columns(part, width):
    return pl.ds(0, width) if part == 0 else pl.ds(0, 512) if part == 1 else pl.ds(512, width - 512)


def kernel(
    tok_hbm, up_hbm, down_hbm, ids_ref, weight_ref, out_ref,
    up_v, down_v, tok, sel, xin, pup, rup, own, act, eout, ret, mix, par, par32, brecv, qs, qr,
    load_sem, far_s, far_r, near_s, near_r, x_s, x_r, rs_s, rs_r, ag_s, ag_r, b_s, b_r, bn_s, bn_r, q_s, q_r,
):
    y = lax.axis_index("sec")
    ep = lax.axis_index("ep")
    core = lax.rem(ep, NC)
    z = lax.rem(ep // NC, NZ)
    x = ep // (NC * NZ)
    width = tok_hbm.shape[1]
    total = tok.shape[1]
    quarter = rup.shape[3]

    def along_z(step):
        return (y, (x * NZ + lax.rem(z + step + NZ, NZ)) * NC + core)

    def in_plane(j):
        return (y, (lax.rem(x + j // NC, NX) * NZ + z) * NC + lax.rem(core + j % NC, NC))

    def along_y(d):
        return (lax.rem(y + d, NY), ep)

    def back(j):
        return ((NX - j // NC) % NX) * NC + j % NC

    def send(src, dst, s, r, to):
        copy = pltpu.make_async_remote_copy(
            src_ref=src, dst_ref=dst, send_sem=s, recv_sem=r, device_id=to, device_id_type=MESH
        )
        copy.start()
        return copy

    def block(o):
        return pl.ds(PLACE[o] * ROWS, ROWS)

    loads = [
        pltpu.make_async_copy(tok_hbm, tok.at[block(0), pl.ds(0, width)], load_sem.at[0]),
        pltpu.make_async_copy(up_hbm, up_v, load_sem.at[1]),
        pltpu.make_async_copy(down_hbm, down_v, load_sem.at[2]),
    ]
    for load in loads:
        load.start()
    barrier = pltpu.get_barrier_semaphore()
    peers = [along_z(s) for s in PEERS_Z] + [in_plane(j) for j in range(1, PLANE)] + [along_y(d) for d in range(1, NY)]
    for peer in peers:
        pl.semaphore_signal(barrier, inc=1, device_id=peer, device_id_type=MESH)

    ids = ids_ref[...]
    lanes = ids.shape[1]
    number = lax.broadcasted_iota(jnp.int32, (128, lanes), 0)
    hits = [number == ids[k : k + 1, :] for k in range(TOP)]
    named = sum(jnp.where(h, 1.0, 0.0) for h in hits).astype(BF16)
    before = lax.broadcasted_iota(jnp.int32, (lanes, lanes), 0) < lax.broadcasted_iota(jnp.int32, (lanes, lanes), 1)
    earlier = jnp.dot(named, jnp.where(before, 1.0, 0.0).astype(BF16), preferred_element_type=F32)
    slot = jnp.concatenate([jnp.sum(jnp.where(h, earlier, 0.0), axis=0, keepdims=True) for h in hits], axis=0)
    code = 2.0 * ids.astype(F32) + slot
    weight = weight_ref[...]
    scale = 2.5 * weight / jnp.sum(weight, axis=0, keepdims=True)
    high = scale.astype(BF16).astype(F32)
    middle = (scale - high).astype(BF16).astype(F32)
    low = scale - high - middle
    table = jnp.concatenate([code, high, middle, low, jnp.zeros((128 - 4 * TOP, lanes), F32)], axis=0).astype(BF16)
    unit = lax.broadcasted_iota(jnp.int32, (ROWS, lanes), 0) == lax.broadcasted_iota(jnp.int32, (ROWS, lanes), 1)
    loads[0].wait()
    tok[block(0), pl.ds(width, total - width)] = lax.dot_general(
        jnp.where(unit, 1.0, 0.0).astype(BF16), table, (((1,), (1,)), ((), ())), preferred_element_type=F32
    ).astype(BF16)

    pl.semaphore_wait(barrier, len(peers))

    far = {}
    for i, a in enumerate(FAR):
        far[a] = send(tok.at[block(0)], tok.at[block(a)], far_s.at[i], far_r.at[i], along_z(a))
    near = {}

    def forward(a):
        for i, (held, b, part) in enumerate(NEAR):
            if held == a:
                cols = columns(part, total)
                near[i] = send(
                    tok.at[block(a), cols], tok.at[block(offset(a, b)), cols], near_s.at[i], near_r.at[i], along_z(b)
                )

    forward(0)
    for a in (3, -3, 6, -6):
        far[a].wait_recv()
        forward(a)

    row = lax.broadcasted_iota(jnp.int32, (128, 128), 0)
    lane = lax.broadcasted_iota(jnp.int32, (128, 128), 1)
    relative = row // (TOP * CAP)
    expert = (lax.rem(x + relative // NC, NX) * NZ + z) * NC + lax.rem(core + lax.rem(relative, NC), NC)
    wanted = (CAP * expert + lax.rem(row, CAP)).astype(F32)
    same = lax.rem(row // CAP, TOP) == lane // ROWS
    turn = jnp.where(row == lane, 1.0, 0.0).astype(BF16)[: 4 * TOP]

    def pick(q):
        codes = lax.dot_general(
            turn, tok[pl.ds(q * 128, 128), pl.ds(width, total - width)], (((1,), (1,)), ((), ())),
            preferred_element_type=F32,
        )
        chosen = jnp.zeros((128, 128), F32)
        scaled = jnp.zeros((128, 128), F32)
        for k in range(TOP):
            match = same & (wanted == codes[k : k + 1, :])
            value = codes[TOP + k : TOP + k + 1, :] + codes[2 * TOP + k : 2 * TOP + k + 1, :]
            value = value + codes[3 * TOP + k : 3 * TOP + k + 1, :]
            chosen = jnp.where(match, 1.0, chosen)
            scaled = jnp.where(match, value, scaled)
        rows = jnp.dot(chosen.astype(BF16), tok[pl.ds(q * 128, 128), pl.ds(0, width)], preferred_element_type=F32)
        sel[q] = rows.astype(BF16)
        xin[q, pl.ds(0, ROWS)] = sel[q, pl.ds(0, ROWS)]
        copies = []
        for j in (4, 5, 2, 6, 3, 7, 1):
            copies.append(
                send(
                    sel.at[q, pl.ds(j * ROWS, ROWS)], xin.at[q, pl.ds(back(j) * ROWS, ROWS)],
                    x_s.at[q, j], x_r.at[q, back(j)], in_plane(j),
                )
            )
        turned = jnp.transpose(scaled)
        first = turned.astype(BF16)
        second = (turned - first.astype(F32)).astype(BF16)
        third = (turned - first.astype(F32) - second.astype(F32)).astype(BF16)
        mix[q, 0] = first
        mix[q, 1] = second
        mix[q, 2] = third
        return copies

    def arrive(q):
        for i, (a, b, _) in enumerate(NEAR):
            if PLACE[offset(a, b)] // 8 == q:
                near[i].wait_recv()

    arrive(0)
    x0 = pick(0)
    arrive(1)
    x1 = pick(1)
    picked = [x0, x1]
    loads[1].wait()
    loads[2].wait()

    sums = [None, None]
    for q in range(2):
        for copy in picked[q]:
            copy.wait_recv()
        sums[q] = []
        for d in (2, 1, 3, 0):
            cols = pl.ds(pl.multiple_of(lax.rem(y + d, NY) * quarter, quarter), quarter)
            part = jnp.dot(xin[q], up_v[:, cols], preferred_element_type=F32)
            if d == 0:
                own[q] = part
            else:
                pup[q, d] = part.astype(BF16)
                sums[q].append(
                    send(pup.at[q, d], rup.at[q, NY - d], rs_s.at[q, d], rs_r.at[q, NY - d], along_y(d))
                )
    gathered = [None, None]
    for q in range(2):
        for copy in sums[q]:
            copy.wait_recv()
        upper = own[q] + rup[q, 1].astype(F32) + rup[q, 2].astype(F32) + rup[q, 3].astype(F32)
        act[q, 0] = (upper / (1.0 + jnp.exp(-upper))).astype(BF16)
        gathered[q] = [
            send(act.at[q, 0], act.at[q, NY - d], ag_s.at[q, d], ag_r.at[q, NY - d], along_y(d)) for d in (2, 1, 3)
        ]
    returned = [None, None]
    for q in range(2):
        for copy in gathered[q]:
            copy.wait_recv()
        result = jnp.zeros((128, width), F32)
        for r in range(NY):
            hidden = pl.ds(pl.multiple_of(lax.rem(y + r, NY) * quarter, quarter), quarter)
            result = result + jnp.dot(act[q, r], down_v[hidden, :], preferred_element_type=F32)
        eout[q] = result.astype(BF16)
        ret[q, pl.ds(0, ROWS)] = eout[q, pl.ds(0, ROWS)]
        returned[q] = [
            send(
                eout.at[q, pl.ds(j * ROWS, ROWS)], ret.at[q, pl.ds(back(j) * ROWS, ROWS)],
                b_s.at[q, j], b_r.at[q, back(j)], in_plane(j),
            )
            for j in (4, 5, 2, 6, 3, 7, 1)
        ]

    homeward = {}
    for q in range(2):
        for copy in returned[q]:
            copy.wait_recv()
        rows = ret[q]
        part = jnp.dot(mix[q, 0], rows, preferred_element_type=F32)
        part = part + jnp.dot(mix[q, 1], rows, preferred_element_type=F32)
        part = part + jnp.dot(mix[q, 2], rows, preferred_element_type=F32)
        par32[q] = part
        par[pl.ds(q * 128, 128)] = part.astype(BF16)
        for i, (a, b, half) in enumerate(NEAR):
            o = offset(a, b)
            if PLACE[o] // 8 == q:
                cols = columns(half, width)
                homeward[i] = send(
                    par.at[block(o), cols], brecv.at[i, :, cols], bn_s.at[i], bn_r.at[i], along_z(-b)
                )
    last = {}
    kept = None
    for a in (6, -6, 3, -3, 0):
        chunk, start = divmod(PLACE[a] * ROWS, 128)
        value = par32[chunk, pl.ds(start, ROWS)]
        for i, (held, b, half) in enumerate(NEAR):
            if held == a:
                homeward[i].wait_recv()
                if half == 0:
                    value = value + brecv[i].astype(F32)
                elif half == 1:
                    value = value + jnp.concatenate(
                        [brecv[i, :, pl.ds(0, 512)].astype(F32), jnp.zeros((ROWS, width - 512), F32)], axis=1
                    )
                else:
                    value = value + jnp.concatenate(
                        [jnp.zeros((ROWS, 512), F32), brecv[i, :, pl.ds(512, width - 512)].astype(F32)], axis=1
                    )
        if a == 0:
            kept = value
        else:
            i = FAR.index(a)
            qs[i] = value.astype(BF16)
            last[a] = send(qs.at[i], qr.at[i], q_s.at[i], q_r.at[i], along_z(-a))
    for a in (3, -3, 6, -6):
        last[a].wait_recv()
        kept = kept + qr[FAR.index(a)].astype(F32)
    out_ref[...] = kept.astype(BF16)

    started = list(far.values()) + list(near.values()) + list(homeward.values()) + list(last.values())
    for group in (picked, sums, gathered, returned):
        started += group[0] + group[1]
    for copy in started:
        copy.wait_send()


def body(tokens, up_weight, down_weight, expert_ids, route_weight):
    width = tokens.shape[1]
    hidden = up_weight.shape[2]
    quarter = hidden // NY
    dma = pltpu.SemaphoreType.DMA
    vmem = pl.BlockSpec(memory_space=pltpu.VMEM)
    anywhere = pl.BlockSpec(memory_space=pl.ANY)
    scratch = [
        pltpu.VMEM((width, hidden), BF16),
        pltpu.VMEM((hidden, width), BF16),
        pltpu.VMEM((256, width + 128), BF16),
        pltpu.VMEM((2, 128, width), BF16),
        pltpu.VMEM((2, 128, width), BF16),
        pltpu.VMEM((2, NY, 128, quarter), BF16),
        pltpu.VMEM((2, NY, 128, quarter), BF16),
        pltpu.VMEM((2, 128, quarter), F32),
        pltpu.VMEM((2, NY, 128, quarter), BF16),
        pltpu.VMEM((2, 128, width), BF16),
        pltpu.VMEM((2, 128, width), BF16),
        pltpu.VMEM((2, 3, 128, 128), BF16),
        pltpu.VMEM((256, width), BF16),
        pltpu.VMEM((2, 128, width), F32),
        pltpu.VMEM((len(NEAR), ROWS, width), BF16),
        pltpu.VMEM((len(FAR), ROWS, width), BF16),
        pltpu.VMEM((len(FAR), ROWS, width), BF16),
        dma((3,)),
        dma((len(FAR),)), dma((len(FAR),)),
        dma((len(NEAR),)), dma((len(NEAR),)),
        dma((2, PLANE)), dma((2, PLANE)),
        dma((2, NY)), dma((2, NY)),
        dma((2, NY)), dma((2, NY)),
        dma((2, PLANE)), dma((2, PLANE)),
        dma((len(NEAR),)), dma((len(NEAR),)),
        dma((len(FAR),)), dma((len(FAR),)),
    ]
    return pl.pallas_call(
        kernel,
        out_shape=jax.ShapeDtypeStruct(tokens.shape, BF16),
        in_specs=[anywhere, anywhere, anywhere, vmem, vmem],
        out_specs=vmem,
        scratch_shapes=scratch,
        compiler_params=pltpu.CompilerParams(
            collective_id=0, has_side_effects=True, vmem_limit_bytes=48 * 2**20
        ),
        cost_estimate=pl.CostEstimate(flops=2 * 2 * 256 * width * hidden, bytes_accessed=4 * width * hidden, transcendentals=0),
        name="experts",
    )(tokens, up_weight[0], down_weight[0], expert_ids.T, route_weight.T)


def solution(mesh):
    placed = (
        P("ep", "sec"),
        P("ep", "sec", None),
        P("ep", None, "sec"),
        P("ep", None),
        P("ep", None),
    )
    return jax.shard_map(
        body, mesh=mesh, in_specs=placed, out_specs=P("ep", "sec"), check_vma=False
    )
```

```python
import functools

import jax
import jax.numpy as jnp
from jax import lax
from jax.experimental import pallas as pl
from jax.experimental.pallas import tpu as pltpu
from jax.sharding import PartitionSpec as P

MESH = pl.DeviceIdType.MESH
F32, BF16 = jnp.float32, jnp.bfloat16
NX, NY, NZ, NC = 4, 4, 16, 2
ROWS, TOP, CAP = 16, 8, 2
PLANE = NX * NC
ORDER = (-4, 5, -5, 6, -6, 7, -7, 8, 0, 1, -1, 3, -3, 2, -2, 4)
PLACE = {o: i for i, o in enumerate(ORDER)}
META = 128
BLOCK_CUT = ((0, 512), (512, 512))
OUT_CUT = ((0, 384), (384, 512))
HOME_CUT = ((0, 512), (512, 384))


def stages(cuts):
    parts = range(len(cuts))
    far = tuple((a, b, s) for a, b in ((0, 3), (0, -3), (3, 3), (-3, -3)) for s in parts)
    near = tuple((a, b, s) for a in (0, 3, -3, 6, -6) for b in (1, -1) for s in parts)
    return far, near + ((6, 2, 0), (-6, -2, 1))


FAR_OUT, NEAR_OUT = stages(BLOCK_CUT)
FAR_HOME, NEAR_HOME = stages(HOME_CUT)
PEERS_Z = (3, -3, 2, -2, 1, -1)
PEERS_PLANE = (4, 5, 2, 6, 3, 7, 1)
PEERS_Y = (2, 1, 3)


def offset(a, b):
    o = a + b
    return 8 if o == -8 else o


def kernel(
    tok_hbm, up_hbm, down_hbm, ids_hbm, weight_hbm, out_ref,
    ids_ref, weight_ref, up_v, down_v, tok, sel, xin, upacc, pup, rup, act, eout, ret, mix, par, par32, brecv, qs, qr,
    load_sem, far_s, far_r, near_s, near_r, x_s, x_r, rs_s, rs_r, ag_s, ag_r, b_s, b_r, bn_s, bn_r, q_s, q_r,
):
    y = lax.axis_index("sec")
    ep = lax.axis_index("ep")
    core = lax.rem(ep, NC)
    z = lax.rem(ep // NC, NZ)
    x = ep // (NC * NZ)
    width = tok_hbm.shape[1]
    quarter = rup.shape[3]
    live = []

    def along_z(step):
        return (y, (x * NZ + lax.rem(z + step + NZ, NZ)) * NC + core)

    def in_plane(j):
        return (y, (lax.rem(x + j // NC, NX) * NZ + z) * NC + lax.rem(core + j % NC, NC))

    def along_y(d):
        return (lax.rem(y + d, NY), ep)

    def back(j):
        return ((NX - j // NC) % NX) * NC + j % NC

    def send(src, dst, s, r, to):
        copy = pltpu.make_async_remote_copy(
            src_ref=src, dst_ref=dst, send_sem=s, recv_sem=r, device_id=to, device_id_type=MESH
        )
        copy.start()
        live.append(copy)
        return copy

    def block(o):
        return pl.ds(PLACE[o] * ROWS, ROWS)

    loads = [
        pltpu.make_async_copy(ids_hbm, ids_ref, load_sem.at[3]),
        pltpu.make_async_copy(weight_hbm, weight_ref, load_sem.at[4]),
        pltpu.make_async_copy(tok_hbm, tok.at[block(0), pl.ds(META, width)], load_sem.at[0]),
        pltpu.make_async_copy(up_hbm, up_v, load_sem.at[1]),
        pltpu.make_async_copy(down_hbm, down_v, load_sem.at[2]),
    ]
    barrier = pltpu.get_barrier_semaphore()
    peers = [along_z(s) for s in PEERS_Z] + [in_plane(j) for j in PEERS_PLANE] + [along_y(d) for d in PEERS_Y]
    for peer in peers:
        pl.semaphore_signal(barrier, inc=1, device_id=peer, device_id_type=MESH)
    for load in loads:
        load.start()

    loads[0].wait()
    loads[1].wait()
    ids = ids_ref[...]
    lanes = ids.shape[1]
    number = lax.broadcasted_iota(jnp.int32, (128, lanes), 0)
    hits = [number == ids[k : k + 1, :] for k in range(TOP)]
    named = sum(jnp.where(h, 1.0, 0.0) for h in hits).astype(BF16)
    before = lax.broadcasted_iota(jnp.int32, (lanes, lanes), 0) < lax.broadcasted_iota(jnp.int32, (lanes, lanes), 1)
    earlier = jnp.dot(named, jnp.where(before, 1.0, 0.0).astype(BF16), preferred_element_type=F32)
    slot = jnp.concatenate([jnp.sum(jnp.where(h, earlier, 0.0), axis=0, keepdims=True) for h in hits], axis=0)
    code = 2.0 * ids.astype(F32) + slot
    weight = weight_ref[...]
    scale = 2.5 * weight / jnp.sum(weight, axis=0, keepdims=True)
    high = scale.astype(BF16).astype(F32)
    middle = (scale - high).astype(BF16).astype(F32)
    low = scale - high - middle
    table = jnp.concatenate([code, high, middle, low, jnp.zeros((META - 4 * TOP, lanes), F32)], axis=0).astype(BF16)
    unit = lax.broadcasted_iota(jnp.int32, (ROWS, lanes), 0) == lax.broadcasted_iota(jnp.int32, (ROWS, lanes), 1)
    tok[block(0), pl.ds(0, META)] = lax.dot_general(
        jnp.where(unit, 1.0, 0.0).astype(BF16), table, (((1,), (1,)), ((), ())), preferred_element_type=F32
    ).astype(BF16)
    loads[2].wait()
    pl.semaphore_wait(barrier, len(peers))

    far, near = {}, {}

    def step(table, i, entry, s_sem, r_sem):
        a, b, s = entry
        cols = pl.ds(*BLOCK_CUT[s])
        table[entry] = send(
            tok.at[block(a), cols], tok.at[block(offset(a, b)), cols], s_sem.at[i], r_sem.at[i], along_z(b)
        )

    def forward(a, s, q):
        for i, entry in enumerate(FAR_OUT):
            if entry[0] == a and entry[2] == s and q == 0:
                step(far, i, entry, far_s, far_r)
        for i, entry in enumerate(NEAR_OUT):
            if entry[0] == a and entry[2] == s and PLACE[offset(entry[0], entry[1])] // 8 == q:
                step(near, i, entry, near_s, near_r)

    def arrive(q, s):
        for entry in NEAR_OUT:
            if PLACE[offset(entry[0], entry[1])] // 8 == q and entry[2] == s:
                near[entry].wait_recv()

    row = lax.broadcasted_iota(jnp.int32, (128, 128), 0)
    lane = lax.broadcasted_iota(jnp.int32, (128, 128), 1)
    relative = row // (TOP * CAP)
    expert = (lax.rem(x + relative // NC, NX) * NZ + z) * NC + lax.rem(core + lax.rem(relative, NC), NC)
    wanted = (CAP * expert + lax.rem(row, CAP)).astype(F32)
    same = lax.rem(row // CAP, TOP) == lane // ROWS
    turn = jnp.where(row == lane, 1.0, 0.0).astype(BF16)[: 4 * TOP]

    def match(q):
        codes = lax.dot_general(
            turn, tok[pl.ds(q * 128, 128), pl.ds(0, META)], (((1,), (1,)), ((), ())), preferred_element_type=F32
        )
        chosen = jnp.zeros((128, 128), F32)
        for k in range(TOP):
            chosen = jnp.where(same & (wanted == codes[k : k + 1, :]), 1.0, chosen)
        return codes, chosen.astype(BF16)

    def pick(q, s, chosen):
        start, size = OUT_CUT[s]
        cols = pl.ds(start, size)
        rows = jnp.dot(chosen, tok[pl.ds(q * 128, 128), pl.ds(META + start, size)], preferred_element_type=F32)
        sel[q, :, cols] = rows.astype(BF16)
        copies = [
            send(
                sel.at[q, pl.ds(j * ROWS, ROWS), cols], xin.at[q, pl.ds(back(j) * ROWS, ROWS), cols],
                x_s.at[q, s, j], x_r.at[q, s, back(j)], in_plane(j),
            )
            for j in PEERS_PLANE
        ]
        xin[q, pl.ds(0, ROWS), cols] = sel[q, pl.ds(0, ROWS), cols]
        return copies

    def weigh(q, codes):
        scaled = jnp.zeros((128, 128), F32)
        for k in range(TOP):
            value = codes[TOP + k : TOP + k + 1, :] + codes[2 * TOP + k : 2 * TOP + k + 1, :]
            value = value + codes[3 * TOP + k : 3 * TOP + k + 1, :]
            scaled = jnp.where(same & (wanted == codes[k : k + 1, :]), value, scaled)
        turned = jnp.transpose(scaled)
        first = turned.astype(BF16)
        second = (turned - first.astype(F32)).astype(BF16)
        third = (turned - first.astype(F32) - second.astype(F32)).astype(BF16)
        mix[q, 0] = first
        mix[q, 1] = second
        mix[q, 2] = third

    parts = range(len(BLOCK_CUT))
    for s in parts:
        forward(0, s, 0)
    for a in (3, 6):
        for s in parts:
            for entry in FAR_OUT:
                if offset(entry[0], entry[1]) in (a, -a) and entry[2] == s:
                    far[entry].wait_recv()
                    forward(offset(entry[0], entry[1]), s, 0)
    for a in (0, 3, -3):
        for s in parts:
            forward(a, s, 1)
    picked = {}
    kept_codes = []
    for q in range(2):
        for s in range(len(BLOCK_CUT)):
            arrive(q, s)
            if s == 0:
                codes, chosen = match(q)
            picked[q, s] = pick(q, s, chosen)
        kept_codes.append(codes)
    loads[3].wait()
    loads[4].wait()

    def tile(d):
        return pl.ds(pl.multiple_of(lax.rem(y + d, NY) * quarter, quarter), quarter)

    sums = [None, None]
    for q in range(2):
        sums[q] = []
        for s, (start, size) in enumerate(OUT_CUT):
            for copy in picked[q, s]:
                copy.wait_recv()
            for d in PEERS_Y + (0,):
                part = jnp.dot(
                    xin[q, :, pl.ds(start, size)], up_v[pl.ds(start, size), tile(d)], preferred_element_type=F32
                )
                if s > 0:
                    part = part + upacc[q, d]
                if s < len(OUT_CUT) - 1 or d == 0:
                    upacc[q, d] = part
                else:
                    pup[q, d] = part.astype(BF16)
                    sums[q].append(
                        send(pup.at[q, d], rup.at[q, NY - d], rs_s.at[q, d], rs_r.at[q, NY - d], along_y(d))
                    )
    for q in range(2):
        weigh(q, kept_codes[q])
    gathered = [None, None]
    for q in range(2):
        for copy in sums[q]:
            copy.wait_recv()
        upper = upacc[q, 0] + rup[q, 1].astype(F32) + rup[q, 2].astype(F32) + rup[q, 3].astype(F32)
        act[q, 0] = (upper / (1.0 + jnp.exp(-upper))).astype(BF16)
        gathered[q] = [
            send(act.at[q, 0], act.at[q, NY - d], ag_s.at[q, d], ag_r.at[q, NY - d], along_y(d)) for d in PEERS_Y
        ]
    returned = {}
    for q in range(2):
        for copy in gathered[q]:
            copy.wait_recv()
        for s in range(len(HOME_CUT)):
            cols = pl.ds(*HOME_CUT[s])
            result = jnp.dot(act[q, 0], down_v[tile(0), cols], preferred_element_type=F32)
            for r in range(1, NY):
                result = result + jnp.dot(act[q, r], down_v[tile(r), cols], preferred_element_type=F32)
            eout[q, :, cols] = result.astype(BF16)
            returned[q, s] = [
                send(
                    eout.at[q, pl.ds(j * ROWS, ROWS), cols], ret.at[q, pl.ds(back(j) * ROWS, ROWS), cols],
                    b_s.at[q, s, j], b_r.at[q, s, back(j)], in_plane(j),
                )
                for j in PEERS_PLANE
            ]
            ret[q, pl.ds(0, ROWS), cols] = eout[q, pl.ds(0, ROWS), cols]

    homeward = {}
    for q in range(2):
        for s in range(len(HOME_CUT)):
            for copy in returned[q, s]:
                copy.wait_recv()
            cols = pl.ds(*HOME_CUT[s])
            rows = ret[q, :, cols]
            part = jnp.dot(mix[q, 0], rows, preferred_element_type=F32)
            part = part + jnp.dot(mix[q, 1], rows, preferred_element_type=F32)
            part = part + jnp.dot(mix[q, 2], rows, preferred_element_type=F32)
            par32[q, :, cols] = part
            par[pl.ds(q * 128, 128), cols] = part.astype(BF16)
            for i, entry in enumerate(NEAR_HOME):
                o = offset(entry[0], entry[1])
                if PLACE[o] // 8 == q and entry[2] == s:
                    homeward[entry] = send(
                        par.at[block(o), cols], brecv.at[i, :, cols], bn_s.at[i], bn_r.at[i], along_z(-entry[1])
                    )
    last = {}

    def group(a, s):
        chunk, start = divmod(PLACE[a] * ROWS, 128)
        cols = pl.ds(*HOME_CUT[s])
        value = par32[chunk, pl.ds(start, ROWS), cols]
        for i, entry in enumerate(NEAR_HOME):
            if entry[0] == a and entry[2] == s:
                homeward[entry].wait_recv()
                value = value + brecv[i, :, cols].astype(F32)
        for i, entry in enumerate(FAR_HOME):
            if entry[0] == a and entry[2] == s:
                last[entry].wait_recv()
                value = value + qr[i, :, cols].astype(F32)
        return value

    def homewards(a, s):
        value = group(a, s)
        cols = pl.ds(*HOME_CUT[s])
        for i, entry in enumerate(FAR_HOME):
            if offset(entry[0], entry[1]) == a and entry[2] == s:
                qs[i, :, cols] = value.astype(BF16)
                last[entry] = send(
                    qs.at[i, :, cols], qr.at[i, :, cols], q_s.at[i], q_r.at[i], along_z(-entry[1])
                )

    for a in sorted({abs(offset(a, b)) for a, b, _ in FAR_HOME}, reverse=True):
        for s in range(len(HOME_CUT)):
            homewards(a, s)
            homewards(-a, s)
    for s in range(len(HOME_CUT)):
        out_ref[:, pl.ds(*HOME_CUT[s])] = group(0, s).astype(BF16)
    for copy in live:
        copy.wait_send()


def body(tokens, up_weight, down_weight, expert_ids, route_weight):
    width = tokens.shape[1]
    hidden = up_weight.shape[2]
    quarter = hidden // NY
    dma = pltpu.SemaphoreType.DMA
    vmem = pl.BlockSpec(memory_space=pltpu.VMEM)
    hbm = pl.BlockSpec(memory_space=pltpu.HBM)
    scratch = [
        pltpu.VMEM((TOP, ROWS), jnp.int32),
        pltpu.VMEM((TOP, ROWS), F32),
        pltpu.VMEM((width, hidden), BF16),
        pltpu.VMEM((hidden, width), BF16),
        pltpu.VMEM((256, META + width), BF16),
        pltpu.VMEM((2, 128, width), BF16),
        pltpu.VMEM((2, 128, width), BF16),
        pltpu.VMEM((2, NY, 128, quarter), F32),
        pltpu.VMEM((2, NY, 128, quarter), BF16),
        pltpu.VMEM((2, NY, 128, quarter), BF16),
        pltpu.VMEM((2, NY, 128, quarter), BF16),
        pltpu.VMEM((2, 128, width), BF16),
        pltpu.VMEM((2, 128, width), BF16),
        pltpu.VMEM((2, 3, 128, 128), BF16),
        pltpu.VMEM((256, width), BF16),
        pltpu.VMEM((2, 128, width), F32),
        pltpu.VMEM((len(NEAR_HOME), ROWS, width), BF16),
        pltpu.VMEM((len(FAR_HOME), ROWS, width), BF16),
        pltpu.VMEM((len(FAR_HOME), ROWS, width), BF16),
        dma((5,)),
        dma((len(FAR_OUT),)), dma((len(FAR_OUT),)),
        dma((len(NEAR_OUT),)), dma((len(NEAR_OUT),)),
        dma((2, 2, PLANE)), dma((2, 2, PLANE)),
        dma((2, NY)), dma((2, NY)),
        dma((2, NY)), dma((2, NY)),
        dma((2, 2, PLANE)), dma((2, 2, PLANE)),
        dma((len(NEAR_HOME),)), dma((len(NEAR_HOME),)),
        dma((len(FAR_HOME),)), dma((len(FAR_HOME),)),
    ]
    return pl.pallas_call(
        kernel,
        out_shape=jax.ShapeDtypeStruct(tokens.shape, BF16),
        in_specs=[hbm] * 5,
        out_specs=vmem,
        scratch_shapes=scratch,
        compiler_params=pltpu.CompilerParams(
            collective_id=0, has_side_effects=True, vmem_limit_bytes=62 * 2**20
        ),
        cost_estimate=pl.CostEstimate(flops=2 * 2 * 256 * width * hidden, bytes_accessed=4 * width * hidden, transcendentals=0),
        name="experts",
    )(tokens, up_weight[0], down_weight[0], expert_ids.T, route_weight.T)


def solution(mesh):
    placed = (
        P("ep", "sec"),
        P("ep", "sec", None),
        P("ep", None, "sec"),
        P("ep", None),
        P("ep", None),
    )
    return jax.shard_map(
        body, mesh=mesh, in_specs=placed, out_specs=P("ep", "sec"), check_vma=False
    )
```

```python
import functools

import jax
import jax.numpy as jnp
from jax import lax
from jax.experimental import pallas as pl
from jax.experimental.pallas import tpu as pltpu
from jax.sharding import PartitionSpec as P

MESH = pl.DeviceIdType.MESH
F32, BF16 = jnp.float32, jnp.bfloat16
NX, NY, NZ, NC = 4, 4, 16, 2
ROWS, TOP, CAP = 16, 8, 2
PLANE = NX * NC
ORDER = (-4, 5, -5, 6, -6, 7, -7, 8, 0, 1, -1, 3, -3, 2, -2, 4)
PLACE = {o: i for i, o in enumerate(ORDER)}
META = 128
HALVES = 2
BLOCK_CUT = ((0, 512), (512, 512))
OUT_CUT = ((0, 384), (384, 512))
HOME_CUT = ((0, 512), (512, 384))


def stages(cuts):
    parts = range(len(cuts))
    far = tuple((a, b, s) for a, b in ((0, 3), (0, -3), (3, 3), (-3, -3)) for s in parts)
    near = tuple((a, b, s) for a in (0, 3, -3, 6, -6) for b in (1, -1) for s in parts)
    return far, near + ((6, 2, 0), (-6, -2, 1))


FAR_OUT, NEAR_OUT = stages(BLOCK_CUT)
FAR_HOME, NEAR_HOME = stages(HOME_CUT)
PEERS_Z = (3, -3, 2, -2, 1, -1)
PEERS_PLANE = (4, 5, 2, 6, 3, 7, 1)
PEERS_Y = (2, 1, 3)


def offset(a, b):
    o = a + b
    return 8 if o == -8 else o


def kernel(
    tok_hbm, up_hbm, down_hbm, ids_hbm, weight_hbm, out_ref,
    ids_ref, weight_ref, up_v, down_v, tok, sel, xin, upacc, pup, rup, act, eout, ret, mix, par, par32, brecv, qs, qr,
    load_sem, far_s, far_r, near_s, near_r, x_s, x_r, rs_s, rs_r, ag_s, ag_r, b_s, b_r, bn_s, bn_r, q_s, q_r,
):
    y = lax.axis_index("sec")
    ep = lax.axis_index("ep")
    core = lax.rem(ep, NC)
    z = lax.rem(ep // NC, NZ)
    x = ep // (NC * NZ)
    width = tok_hbm.shape[1]
    quarter = rup.shape[3]
    live = []

    def along_z(step):
        return (y, (x * NZ + lax.rem(z + step + NZ, NZ)) * NC + core)

    def in_plane(j):
        return (y, (lax.rem(x + j // NC, NX) * NZ + z) * NC + lax.rem(core + j % NC, NC))

    def along_y(d):
        return (lax.rem(y + d, NY), ep)

    def back(j):
        return ((NX - j // NC) % NX) * NC + j % NC

    def send(src, dst, s, r, to):
        copy = pltpu.make_async_remote_copy(
            src_ref=src, dst_ref=dst, send_sem=s, recv_sem=r, device_id=to, device_id_type=MESH
        )
        copy.start()
        live.append(copy)
        return copy

    def block(o):
        return pl.ds(PLACE[o] * ROWS, ROWS)

    loads = [
        pltpu.make_async_copy(ids_hbm, ids_ref, load_sem.at[3]),
        pltpu.make_async_copy(weight_hbm, weight_ref, load_sem.at[4]),
        pltpu.make_async_copy(tok_hbm, tok.at[block(0), pl.ds(META, width)], load_sem.at[0]),
        pltpu.make_async_copy(up_hbm, up_v, load_sem.at[1]),
        pltpu.make_async_copy(down_hbm, down_v, load_sem.at[2]),
    ]
    barrier = pltpu.get_barrier_semaphore()
    peers = [along_z(s) for s in PEERS_Z] + [in_plane(j) for j in PEERS_PLANE] + [along_y(d) for d in PEERS_Y]
    for peer in peers:
        pl.semaphore_signal(barrier, inc=1, device_id=peer, device_id_type=MESH)
    for load in loads:
        load.start()

    loads[0].wait()
    loads[1].wait()
    ids = ids_ref[...]
    lanes = ids.shape[1]
    number = lax.broadcasted_iota(jnp.int32, (128, lanes), 0)
    hits = [number == ids[k : k + 1, :] for k in range(TOP)]
    named = sum(jnp.where(h, 1.0, 0.0) for h in hits).astype(BF16)
    before = lax.broadcasted_iota(jnp.int32, (lanes, lanes), 0) < lax.broadcasted_iota(jnp.int32, (lanes, lanes), 1)
    earlier = jnp.dot(named, jnp.where(before, 1.0, 0.0).astype(BF16), preferred_element_type=F32)
    slot = jnp.concatenate([jnp.sum(jnp.where(h, earlier, 0.0), axis=0, keepdims=True) for h in hits], axis=0)
    code = 2.0 * ids.astype(F32) + slot
    weight = weight_ref[...]
    scale = 2.5 * weight / jnp.sum(weight, axis=0, keepdims=True)
    high = scale.astype(BF16).astype(F32)
    middle = (scale - high).astype(BF16).astype(F32)
    low = scale - high - middle
    table = jnp.concatenate([code, high, middle, low, jnp.zeros((META - 4 * TOP, lanes), F32)], axis=0).astype(BF16)
    unit = lax.broadcasted_iota(jnp.int32, (ROWS, lanes), 0) == lax.broadcasted_iota(jnp.int32, (ROWS, lanes), 1)
    tok[block(0), pl.ds(0, META)] = lax.dot_general(
        jnp.where(unit, 1.0, 0.0).astype(BF16), table, (((1,), (1,)), ((), ())), preferred_element_type=F32
    ).astype(BF16)
    loads[2].wait()
    pl.semaphore_wait(barrier, len(peers))

    far, near = {}, {}

    def step(table, i, entry, s_sem, r_sem):
        a, b, s = entry
        cols = pl.ds(*BLOCK_CUT[s])
        table[entry] = send(
            tok.at[block(a), cols], tok.at[block(offset(a, b)), cols], s_sem.at[i], r_sem.at[i], along_z(b)
        )

    def forward(a, s, q):
        for i, entry in enumerate(FAR_OUT):
            if entry[0] == a and entry[2] == s and q == 0:
                step(far, i, entry, far_s, far_r)
        for i, entry in enumerate(NEAR_OUT):
            if entry[0] == a and entry[2] == s and PLACE[offset(entry[0], entry[1])] // 8 == q:
                step(near, i, entry, near_s, near_r)

    def arrive(q, s):
        for entry in NEAR_OUT:
            if PLACE[offset(entry[0], entry[1])] // 8 == q and entry[2] == s:
                near[entry].wait_recv()

    row = lax.broadcasted_iota(jnp.int32, (128, 128), 0)
    lane = lax.broadcasted_iota(jnp.int32, (128, 128), 1)
    relative = row // (TOP * CAP)
    expert = (lax.rem(x + relative // NC, NX) * NZ + z) * NC + lax.rem(core + lax.rem(relative, NC), NC)
    wanted = (CAP * expert + lax.rem(row, CAP)).astype(F32)
    same = lax.rem(row // CAP, TOP) == lane // ROWS
    turn = jnp.where(row == lane, 1.0, 0.0).astype(BF16)[: 4 * TOP]

    def match(q):
        codes = lax.dot_general(
            turn, tok[pl.ds(q * 128, 128), pl.ds(0, META)], (((1,), (1,)), ((), ())), preferred_element_type=F32
        )
        chosen = jnp.zeros((128, 128), F32)
        for k in range(TOP):
            chosen = jnp.where(same & (wanted == codes[k : k + 1, :]), 1.0, chosen)
        return codes, chosen.astype(BF16)

    def pick(q, s, chosen):
        start, size = OUT_CUT[s]
        cols = pl.ds(start, size)
        rows = jnp.dot(chosen, tok[pl.ds(q * 128, 128), pl.ds(META + start, size)], preferred_element_type=F32)
        sel[q, :, cols] = rows.astype(BF16)
        copies = [
            send(
                sel.at[q, pl.ds(j * ROWS, ROWS), cols], xin.at[q, pl.ds(back(j) * ROWS, ROWS), cols],
                x_s.at[q, s, j], x_r.at[q, s, back(j)], in_plane(j),
            )
            for j in PEERS_PLANE
        ]
        xin[q, pl.ds(0, ROWS), cols] = sel[q, pl.ds(0, ROWS), cols]
        return copies

    def weigh(q, codes):
        scaled = jnp.zeros((128, 128), F32)
        for k in range(TOP):
            value = codes[TOP + k : TOP + k + 1, :] + codes[2 * TOP + k : 2 * TOP + k + 1, :]
            value = value + codes[3 * TOP + k : 3 * TOP + k + 1, :]
            scaled = jnp.where(same & (wanted == codes[k : k + 1, :]), value, scaled)
        turned = jnp.transpose(scaled)
        first = turned.astype(BF16)
        second = (turned - first.astype(F32)).astype(BF16)
        third = (turned - first.astype(F32) - second.astype(F32)).astype(BF16)
        mix[q, 0] = first
        mix[q, 1] = second
        mix[q, 2] = third

    parts = range(len(BLOCK_CUT))
    for s in parts:
        forward(0, s, 0)
    for a in (3, 6):
        for s in parts:
            for entry in FAR_OUT:
                if offset(entry[0], entry[1]) in (a, -a) and entry[2] == s:
                    far[entry].wait_recv()
                    forward(offset(entry[0], entry[1]), s, 0)
    for a in (0, 3, -3):
        for s in parts:
            forward(a, s, 1)
    picked = {}
    kept_codes = []
    for q in range(2):
        for s in range(len(BLOCK_CUT)):
            arrive(q, s)
            if s == 0:
                codes, chosen = match(q)
            picked[q, s] = pick(q, s, chosen)
        kept_codes.append(codes)
    loads[3].wait()
    loads[4].wait()

    def tile(d):
        return pl.ds(pl.multiple_of(lax.rem(y + d, NY) * quarter, quarter), quarter)

    half = xin.shape[1] // HALVES
    sums = {}
    for q in range(2):
        for s, (start, size) in enumerate(OUT_CUT):
            for copy in picked[q, s]:
                copy.wait_recv()
            for d in PEERS_Y + (0,):
                part = jnp.dot(
                    xin[q, :, pl.ds(start, size)], up_v[pl.ds(start, size), tile(d)], preferred_element_type=F32
                )
                if s > 0:
                    part = part + upacc[q, d]
                if s < len(OUT_CUT) - 1 or d == 0:
                    upacc[q, d] = part
                else:
                    pup[q, d] = part.astype(BF16)
        for h in range(HALVES):
            rows = pl.ds(h * half, half)
            for d in PEERS_Y:
                sums[q, h, d] = send(
                    pup.at[q, d, rows], rup.at[q, NY - d, rows], rs_s.at[q, h, d], rs_r.at[q, h, NY - d], along_y(d)
                )
    for q in range(2):
        weigh(q, kept_codes[q])
    gathered = [[], []]
    for q in range(2):
        for h in range(HALVES):
            rows = pl.ds(h * half, half)
            for d in PEERS_Y:
                sums[q, h, d].wait_recv()
            upper = upacc[q, 0, rows]
            for r in range(1, NY):
                upper = upper + rup[q, r, rows].astype(F32)
            act[q, 0, rows] = (upper / (1.0 + jnp.exp(-upper))).astype(BF16)
            gathered[q] += [
                send(
                    act.at[q, 0, rows], act.at[q, NY - d, rows], ag_s.at[q, h, d], ag_r.at[q, h, NY - d], along_y(d)
                )
                for d in PEERS_Y
            ]
    returned = {}
    for q in range(2):
        for copy in gathered[q]:
            copy.wait_recv()
        for s in range(len(HOME_CUT)):
            cols = pl.ds(*HOME_CUT[s])
            result = jnp.dot(act[q, 0], down_v[tile(0), cols], preferred_element_type=F32)
            for r in range(1, NY):
                result = result + jnp.dot(act[q, r], down_v[tile(r), cols], preferred_element_type=F32)
            eout[q, :, cols] = result.astype(BF16)
            returned[q, s] = [
                send(
                    eout.at[q, pl.ds(j * ROWS, ROWS), cols], ret.at[q, pl.ds(back(j) * ROWS, ROWS), cols],
                    b_s.at[q, s, j], b_r.at[q, s, back(j)], in_plane(j),
                )
                for j in PEERS_PLANE
            ]
            ret[q, pl.ds(0, ROWS), cols] = eout[q, pl.ds(0, ROWS), cols]

    homeward = {}
    for q in range(2):
        for s in range(len(HOME_CUT)):
            for copy in returned[q, s]:
                copy.wait_recv()
            cols = pl.ds(*HOME_CUT[s])
            rows = ret[q, :, cols]
            part = jnp.dot(mix[q, 0], rows, preferred_element_type=F32)
            part = part + jnp.dot(mix[q, 1], rows, preferred_element_type=F32)
            part = part + jnp.dot(mix[q, 2], rows, preferred_element_type=F32)
            par32[q, :, cols] = part
            par[pl.ds(q * 128, 128), cols] = part.astype(BF16)
            for i, entry in enumerate(NEAR_HOME):
                o = offset(entry[0], entry[1])
                if PLACE[o] // 8 == q and entry[2] == s:
                    homeward[entry] = send(
                        par.at[block(o), cols], brecv.at[i, :, cols], bn_s.at[i], bn_r.at[i], along_z(-entry[1])
                    )
    last = {}

    def group(a, s):
        chunk, start = divmod(PLACE[a] * ROWS, 128)
        cols = pl.ds(*HOME_CUT[s])
        value = par32[chunk, pl.ds(start, ROWS), cols]
        for i, entry in enumerate(NEAR_HOME):
            if entry[0] == a and entry[2] == s:
                homeward[entry].wait_recv()
                value = value + brecv[i, :, cols].astype(F32)
        for i, entry in enumerate(FAR_HOME):
            if entry[0] == a and entry[2] == s:
                last[entry].wait_recv()
                value = value + qr[i, :, cols].astype(F32)
        return value

    def homewards(a, s):
        value = group(a, s)
        cols = pl.ds(*HOME_CUT[s])
        for i, entry in enumerate(FAR_HOME):
            if offset(entry[0], entry[1]) == a and entry[2] == s:
                qs[i, :, cols] = value.astype(BF16)
                last[entry] = send(
                    qs.at[i, :, cols], qr.at[i, :, cols], q_s.at[i], q_r.at[i], along_z(-entry[1])
                )

    for a in sorted({abs(offset(a, b)) for a, b, _ in FAR_HOME}, reverse=True):
        for s in range(len(HOME_CUT)):
            homewards(a, s)
            homewards(-a, s)
    for s in range(len(HOME_CUT)):
        out_ref[:, pl.ds(*HOME_CUT[s])] = group(0, s).astype(BF16)
    for copy in live:
        copy.wait_send()


def body(tokens, up_weight, down_weight, expert_ids, route_weight):
    width = tokens.shape[1]
    hidden = up_weight.shape[2]
    quarter = hidden // NY
    dma = pltpu.SemaphoreType.DMA
    vmem = pl.BlockSpec(memory_space=pltpu.VMEM)
    hbm = pl.BlockSpec(memory_space=pltpu.HBM)
    scratch = [
        pltpu.VMEM((TOP, ROWS), jnp.int32),
        pltpu.VMEM((TOP, ROWS), F32),
        pltpu.VMEM((width, hidden), BF16),
        pltpu.VMEM((hidden, width), BF16),
        pltpu.VMEM((256, META + width), BF16),
        pltpu.VMEM((2, 128, width), BF16),
        pltpu.VMEM((2, 128, width), BF16),
        pltpu.VMEM((2, NY, 128, quarter), F32),
        pltpu.VMEM((2, NY, 128, quarter), BF16),
        pltpu.VMEM((2, NY, 128, quarter), BF16),
        pltpu.VMEM((2, NY, 128, quarter), BF16),
        pltpu.VMEM((2, 128, width), BF16),
        pltpu.VMEM((2, 128, width), BF16),
        pltpu.VMEM((2, 3, 128, 128), BF16),
        pltpu.VMEM((256, width), BF16),
        pltpu.VMEM((2, 128, width), F32),
        pltpu.VMEM((len(NEAR_HOME), ROWS, width), BF16),
        pltpu.VMEM((len(FAR_HOME), ROWS, width), BF16),
        pltpu.VMEM((len(FAR_HOME), ROWS, width), BF16),
        dma((5,)),
        dma((len(FAR_OUT),)), dma((len(FAR_OUT),)),
        dma((len(NEAR_OUT),)), dma((len(NEAR_OUT),)),
        dma((2, 2, PLANE)), dma((2, 2, PLANE)),
        dma((2, HALVES, NY)), dma((2, HALVES, NY)),
        dma((2, HALVES, NY)), dma((2, HALVES, NY)),
        dma((2, 2, PLANE)), dma((2, 2, PLANE)),
        dma((len(NEAR_HOME),)), dma((len(NEAR_HOME),)),
        dma((len(FAR_HOME),)), dma((len(FAR_HOME),)),
    ]
    return pl.pallas_call(
        kernel,
        out_shape=pltpu.VMEM(tokens.shape, BF16),
        in_specs=[hbm] * 5,
        out_specs=vmem,
        scratch_shapes=scratch,
        compiler_params=pltpu.CompilerParams(
            collective_id=0, has_side_effects=True, vmem_limit_bytes=62 * 2**20
        ),
        cost_estimate=pl.CostEstimate(flops=2 * 2 * 256 * width * hidden, bytes_accessed=4 * width * hidden, transcendentals=0),
        name="experts",
    )(tokens, up_weight[0], down_weight[0], expert_ids.T, route_weight.T)


def solution(mesh):
    placed = (
        P("ep", "sec"),
        P("ep", "sec", None),
        P("ep", None, "sec"),
        P("ep", None),
        P("ep", None),
    )
    return jax.shard_map(
        body, mesh=mesh, in_specs=placed, out_specs=P("ep", "sec"), check_vma=False
    )
```

```python
import functools

import jax
import jax.numpy as jnp
from jax import lax
from jax.experimental import pallas as pl
from jax.experimental.pallas import tpu as pltpu
from jax.sharding import PartitionSpec as P

MESH = pl.DeviceIdType.MESH
F32, BF16 = jnp.float32, jnp.bfloat16
NX, NY, NZ, NC = 4, 4, 16, 2
ROWS, TOP, CAP = 16, 8, 2
PLANE = NX * NC
ORDER = (-4, 5, -5, 6, -6, 7, -7, 8, 0, 1, -1, 3, -3, 2, -2, 4)
PLACE = {o: i for i, o in enumerate(ORDER)}
META = 128
HALVES = 2
BLOCK_CUT = ((0, 512), (512, 512))
OUT_CUT = ((0, 384), (384, 512))
HOME_CUT = ((0, 512), (512, 384))


def stages(cuts):
    parts = range(len(cuts))
    far = tuple((a, b, s) for a, b in ((0, 3), (0, -3), (3, 3), (-3, -3)) for s in parts)
    near = tuple((a, b, s) for a in (0, 3, -3, 6, -6) for b in (1, -1) for s in parts)
    return far, near + ((6, 2, 0), (-6, -2, 1))


FAR_OUT, NEAR_OUT = stages(BLOCK_CUT)
FAR_HOME, NEAR_HOME = stages(HOME_CUT)
PEERS_Z = (3, -3, 2, -2, 1, -1)
PEERS_PLANE = (4, 5, 2, 6, 3, 7, 1)
PEERS_Y = (2, 1, 3)


def offset(a, b):
    o = a + b
    return 8 if o == -8 else o


def kernel(
    tok_hbm, up_hbm, down_hbm, ids_hbm, weight_hbm, out_ref,
    ids_ref, weight_ref, up_v, down_v, tok, sel, xin, upacc, pup, rup, act, eout, ret, mix, par, par32, brecv, qs, qr,
    load_sem, far_s, far_r, near_s, near_r, x_s, x_r, rs_s, rs_r, ag_s, ag_r, b_s, b_r, bn_s, bn_r, q_s, q_r,
):
    y = lax.axis_index("sec")
    ep = lax.axis_index("ep")
    core = lax.rem(ep, NC)
    z = lax.rem(ep // NC, NZ)
    x = ep // (NC * NZ)
    width = tok_hbm.shape[1]
    quarter = rup.shape[3]
    live = []

    def along_z(step):
        return (y, (x * NZ + lax.rem(z + step + NZ, NZ)) * NC + core)

    def in_plane(j):
        return (y, (lax.rem(x + j // NC, NX) * NZ + z) * NC + lax.rem(core + j % NC, NC))

    def along_y(d):
        return (lax.rem(y + d, NY), ep)

    def back(j):
        return ((NX - j // NC) % NX) * NC + j % NC

    def send(src, dst, s, r, to):
        copy = pltpu.make_async_remote_copy(
            src_ref=src, dst_ref=dst, send_sem=s, recv_sem=r, device_id=to, device_id_type=MESH
        )
        copy.start()
        live.append(copy)
        return copy

    def block(o):
        return pl.ds(PLACE[o] * ROWS, ROWS)

    loads = [
        pltpu.make_async_copy(ids_hbm, ids_ref, load_sem.at[3]),
        pltpu.make_async_copy(weight_hbm, weight_ref, load_sem.at[4]),
        pltpu.make_async_copy(tok_hbm, tok.at[block(0), pl.ds(META, width)], load_sem.at[0]),
        pltpu.make_async_copy(up_hbm, up_v, load_sem.at[1]),
        pltpu.make_async_copy(down_hbm, down_v, load_sem.at[2]),
    ]
    barrier = pltpu.get_barrier_semaphore()
    peers = [along_z(s) for s in PEERS_Z] + [in_plane(j) for j in PEERS_PLANE] + [along_y(d) for d in PEERS_Y]
    for peer in peers:
        pl.semaphore_signal(barrier, inc=1, device_id=peer, device_id_type=MESH)
    for load in loads[:3]:
        load.start()

    loads[0].wait()
    loads[1].wait()
    ids = ids_ref[...]
    lanes = ids.shape[1]
    number = lax.broadcasted_iota(jnp.int32, (128, lanes), 0)
    hits = [number == ids[k : k + 1, :] for k in range(TOP)]
    named = sum(jnp.where(h, 1.0, 0.0) for h in hits).astype(BF16)
    before = lax.broadcasted_iota(jnp.int32, (lanes, lanes), 0) < lax.broadcasted_iota(jnp.int32, (lanes, lanes), 1)
    earlier = jnp.dot(named, jnp.where(before, 1.0, 0.0).astype(BF16), preferred_element_type=F32)
    slot = jnp.concatenate([jnp.sum(jnp.where(h, earlier, 0.0), axis=0, keepdims=True) for h in hits], axis=0)
    code = 2.0 * ids.astype(F32) + slot
    weight = weight_ref[...]
    scale = 2.5 * weight / jnp.sum(weight, axis=0, keepdims=True)
    high = scale.astype(BF16).astype(F32)
    middle = (scale - high).astype(BF16).astype(F32)
    low = scale - high - middle
    table = jnp.concatenate([code, high, middle, low, jnp.zeros((META - 4 * TOP, lanes), F32)], axis=0).astype(BF16)
    unit = lax.broadcasted_iota(jnp.int32, (ROWS, lanes), 0) == lax.broadcasted_iota(jnp.int32, (ROWS, lanes), 1)
    tok[block(0), pl.ds(0, META)] = lax.dot_general(
        jnp.where(unit, 1.0, 0.0).astype(BF16), table, (((1,), (1,)), ((), ())), preferred_element_type=F32
    ).astype(BF16)
    loads[2].wait()
    for load in loads[3:]:
        load.start()
    pl.semaphore_wait(barrier, len(peers))

    far, near = {}, {}

    def step(table, i, entry, s_sem, r_sem):
        a, b, s = entry
        cols = pl.ds(*BLOCK_CUT[s])
        table[entry] = send(
            tok.at[block(a), cols], tok.at[block(offset(a, b)), cols], s_sem.at[i], r_sem.at[i], along_z(b)
        )

    def forward(a, s, q):
        for i, entry in enumerate(FAR_OUT):
            if entry[0] == a and entry[2] == s and q == 0:
                step(far, i, entry, far_s, far_r)
        for i, entry in enumerate(NEAR_OUT):
            if entry[0] == a and entry[2] == s and PLACE[offset(entry[0], entry[1])] // 8 == q:
                step(near, i, entry, near_s, near_r)

    def arrive(q, s):
        for entry in NEAR_OUT:
            if PLACE[offset(entry[0], entry[1])] // 8 == q and entry[2] == s:
                near[entry].wait_recv()

    row = lax.broadcasted_iota(jnp.int32, (128, 128), 0)
    lane = lax.broadcasted_iota(jnp.int32, (128, 128), 1)
    relative = row // (TOP * CAP)
    expert = (lax.rem(x + relative // NC, NX) * NZ + z) * NC + lax.rem(core + lax.rem(relative, NC), NC)
    wanted = (CAP * expert + lax.rem(row, CAP)).astype(F32)
    same = lax.rem(row // CAP, TOP) == lane // ROWS
    turn = jnp.where(row == lane, 1.0, 0.0).astype(BF16)[: 4 * TOP]

    def match(q):
        codes = lax.dot_general(
            turn, tok[pl.ds(q * 128, 128), pl.ds(0, META)], (((1,), (1,)), ((), ())), preferred_element_type=F32
        )
        chosen = jnp.zeros((128, 128), F32)
        for k in range(TOP):
            chosen = jnp.where(same & (wanted == codes[k : k + 1, :]), 1.0, chosen)
        return codes, chosen.astype(BF16)

    def pick(q, s, chosen):
        start, size = OUT_CUT[s]
        cols = pl.ds(start, size)
        rows = jnp.dot(chosen, tok[pl.ds(q * 128, 128), pl.ds(META + start, size)], preferred_element_type=F32)
        sel[q, :, cols] = rows.astype(BF16)
        copies = [
            send(
                sel.at[q, pl.ds(j * ROWS, ROWS), cols], xin.at[q, pl.ds(back(j) * ROWS, ROWS), cols],
                x_s.at[q, s, j], x_r.at[q, s, back(j)], in_plane(j),
            )
            for j in PEERS_PLANE
        ]
        xin[q, pl.ds(0, ROWS), cols] = sel[q, pl.ds(0, ROWS), cols]
        return copies

    def weigh(q, codes):
        scaled = jnp.zeros((128, 128), F32)
        for k in range(TOP):
            value = codes[TOP + k : TOP + k + 1, :] + codes[2 * TOP + k : 2 * TOP + k + 1, :]
            value = value + codes[3 * TOP + k : 3 * TOP + k + 1, :]
            scaled = jnp.where(same & (wanted == codes[k : k + 1, :]), value, scaled)
        turned = jnp.transpose(scaled)
        first = turned.astype(BF16)
        second = (turned - first.astype(F32)).astype(BF16)
        third = (turned - first.astype(F32) - second.astype(F32)).astype(BF16)
        mix[q, 0] = first
        mix[q, 1] = second
        mix[q, 2] = third

    parts = range(len(BLOCK_CUT))
    for s in parts:
        forward(0, s, 0)
    for a in (3, 6):
        for s in parts:
            for entry in FAR_OUT:
                if offset(entry[0], entry[1]) in (a, -a) and entry[2] == s:
                    far[entry].wait_recv()
                    forward(offset(entry[0], entry[1]), s, 0)
    for a in (0, 3, -3):
        for s in parts:
            forward(a, s, 1)
    picked = {}
    kept_codes = []
    for q in range(2):
        for s in range(len(BLOCK_CUT)):
            arrive(q, s)
            if s == 0:
                codes, chosen = match(q)
            picked[q, s] = pick(q, s, chosen)
        kept_codes.append(codes)
    loads[3].wait()
    loads[4].wait()

    def tile(d):
        return pl.ds(pl.multiple_of(lax.rem(y + d, NY) * quarter, quarter), quarter)

    half = xin.shape[1] // HALVES
    sums = {}
    for q in range(2):
        for s, (start, size) in enumerate(OUT_CUT):
            for copy in picked[q, s]:
                copy.wait_recv()
            for d in PEERS_Y + (0,):
                part = jnp.dot(
                    xin[q, :, pl.ds(start, size)], up_v[pl.ds(start, size), tile(d)], preferred_element_type=F32
                )
                if s > 0:
                    part = part + upacc[q, d]
                if s < len(OUT_CUT) - 1 or d == 0:
                    upacc[q, d] = part
                else:
                    pup[q, d] = part.astype(BF16)
        for h in range(HALVES):
            rows = pl.ds(h * half, half)
            for d in PEERS_Y:
                sums[q, h, d] = send(
                    pup.at[q, d, rows], rup.at[q, NY - d, rows], rs_s.at[q, h, d], rs_r.at[q, h, NY - d], along_y(d)
                )
    for q in range(2):
        weigh(q, kept_codes[q])
    gathered = [[], []]
    for q in range(2):
        for h in range(HALVES):
            rows = pl.ds(h * half, half)
            for d in PEERS_Y:
                sums[q, h, d].wait_recv()
            upper = upacc[q, 0, rows]
            for r in range(1, NY):
                upper = upper + rup[q, r, rows].astype(F32)
            act[q, 0, rows] = (upper / (1.0 + jnp.exp(-upper))).astype(BF16)
            gathered[q] += [
                send(
                    act.at[q, 0, rows], act.at[q, NY - d, rows], ag_s.at[q, h, d], ag_r.at[q, h, NY - d], along_y(d)
                )
                for d in PEERS_Y
            ]
    returned = {}
    for q in range(2):
        for copy in gathered[q]:
            copy.wait_recv()
        for s in range(len(HOME_CUT)):
            cols = pl.ds(*HOME_CUT[s])
            result = jnp.dot(act[q, 0], down_v[tile(0), cols], preferred_element_type=F32)
            for r in range(1, NY):
                result = result + jnp.dot(act[q, r], down_v[tile(r), cols], preferred_element_type=F32)
            eout[q, :, cols] = result.astype(BF16)
            returned[q, s] = [
                send(
                    eout.at[q, pl.ds(j * ROWS, ROWS), cols], ret.at[q, pl.ds(back(j) * ROWS, ROWS), cols],
                    b_s.at[q, s, j], b_r.at[q, s, back(j)], in_plane(j),
                )
                for j in PEERS_PLANE
            ]
            ret[q, pl.ds(0, ROWS), cols] = eout[q, pl.ds(0, ROWS), cols]

    homeward = {}
    for q in range(2):
        for s in range(len(HOME_CUT)):
            for copy in returned[q, s]:
                copy.wait_recv()
            cols = pl.ds(*HOME_CUT[s])
            rows = ret[q, :, cols]
            part = jnp.dot(mix[q, 0], rows, preferred_element_type=F32)
            part = part + jnp.dot(mix[q, 1], rows, preferred_element_type=F32)
            part = part + jnp.dot(mix[q, 2], rows, preferred_element_type=F32)
            par32[q, :, cols] = part
            par[pl.ds(q * 128, 128), cols] = part.astype(BF16)
            for i, entry in enumerate(NEAR_HOME):
                o = offset(entry[0], entry[1])
                if PLACE[o] // 8 == q and entry[2] == s:
                    homeward[entry] = send(
                        par.at[block(o), cols], brecv.at[i, :, cols], bn_s.at[i], bn_r.at[i], along_z(-entry[1])
                    )
    last = {}

    def group(a, s):
        chunk, start = divmod(PLACE[a] * ROWS, 128)
        cols = pl.ds(*HOME_CUT[s])
        value = par32[chunk, pl.ds(start, ROWS), cols]
        for i, entry in enumerate(NEAR_HOME):
            if entry[0] == a and entry[2] == s:
                homeward[entry].wait_recv()
                value = value + brecv[i, :, cols].astype(F32)
        for i, entry in enumerate(FAR_HOME):
            if entry[0] == a and entry[2] == s:
                last[entry].wait_recv()
                value = value + qr[i, :, cols].astype(F32)
        return value

    def homewards(a, s):
        value = group(a, s)
        cols = pl.ds(*HOME_CUT[s])
        for i, entry in enumerate(FAR_HOME):
            if offset(entry[0], entry[1]) == a and entry[2] == s:
                qs[i, :, cols] = value.astype(BF16)
                last[entry] = send(
                    qs.at[i, :, cols], qr.at[i, :, cols], q_s.at[i], q_r.at[i], along_z(-entry[1])
                )

    for a in sorted({abs(offset(a, b)) for a, b, _ in FAR_HOME}, reverse=True):
        for s in range(len(HOME_CUT)):
            homewards(a, s)
            homewards(-a, s)
    for copy in live[: -len(FAR_HOME) // 2]:
        copy.wait_send()
    for s in range(len(HOME_CUT)):
        out_ref[:, pl.ds(*HOME_CUT[s])] = group(0, s).astype(BF16)
    for copy in live[-len(FAR_HOME) // 2 :]:
        copy.wait_send()


def body(tokens, up_weight, down_weight, expert_ids, route_weight):
    width = tokens.shape[1]
    hidden = up_weight.shape[2]
    quarter = hidden // NY
    dma = pltpu.SemaphoreType.DMA
    vmem = pl.BlockSpec(memory_space=pltpu.VMEM)
    hbm = pl.BlockSpec(memory_space=pltpu.HBM)
    scratch = [
        pltpu.VMEM((TOP, ROWS), jnp.int32),
        pltpu.VMEM((TOP, ROWS), F32),
        pltpu.VMEM((width, hidden), BF16),
        pltpu.VMEM((hidden, width), BF16),
        pltpu.VMEM((256, META + width), BF16),
        pltpu.VMEM((2, 128, width), BF16),
        pltpu.VMEM((2, 128, width), BF16),
        pltpu.VMEM((2, NY, 128, quarter), F32),
        pltpu.VMEM((2, NY, 128, quarter), BF16),
        pltpu.VMEM((2, NY, 128, quarter), BF16),
        pltpu.VMEM((2, NY, 128, quarter), BF16),
        pltpu.VMEM((2, 128, width), BF16),
        pltpu.VMEM((2, 128, width), BF16),
        pltpu.VMEM((2, 3, 128, 128), BF16),
        pltpu.VMEM((256, width), BF16),
        pltpu.VMEM((2, 128, width), F32),
        pltpu.VMEM((len(NEAR_HOME), ROWS, width), BF16),
        pltpu.VMEM((len(FAR_HOME), ROWS, width), BF16),
        pltpu.VMEM((len(FAR_HOME), ROWS, width), BF16),
        dma((5,)),
        dma((len(FAR_OUT),)), dma((len(FAR_OUT),)),
        dma((len(NEAR_OUT),)), dma((len(NEAR_OUT),)),
        dma((2, 2, PLANE)), dma((2, 2, PLANE)),
        dma((2, HALVES, NY)), dma((2, HALVES, NY)),
        dma((2, HALVES, NY)), dma((2, HALVES, NY)),
        dma((2, 2, PLANE)), dma((2, 2, PLANE)),
        dma((len(NEAR_HOME),)), dma((len(NEAR_HOME),)),
        dma((len(FAR_HOME),)), dma((len(FAR_HOME),)),
    ]
    return pl.pallas_call(
        kernel,
        out_shape=pltpu.VMEM(tokens.shape, BF16),
        in_specs=[hbm] * 5,
        out_specs=vmem,
        scratch_shapes=scratch,
        compiler_params=pltpu.CompilerParams(
            collective_id=0, has_side_effects=True, vmem_limit_bytes=62 * 2**20
        ),
        cost_estimate=pl.CostEstimate(flops=2 * 2 * 256 * width * hidden, bytes_accessed=4 * width * hidden, transcendentals=0),
        name="experts",
    )(tokens, up_weight[0], down_weight[0], expert_ids.T, route_weight.T)


def solution(mesh):
    placed = (
        P("ep", "sec"),
        P("ep", "sec", None),
        P("ep", None, "sec"),
        P("ep", None),
        P("ep", None),
    )
    return jax.shard_map(
        body, mesh=mesh, in_specs=placed, out_specs=P("ep", "sec"), check_vma=False
    )
```
